32 devices in a mesh: win: 2 (over x), chan: 16 (over z, y, core).
Axes of the slice: x: 2, y: 2, z: 4, core: 2. Of those that a mesh axis runs over, the one named last changes fastest.
Arguments:
- spectra: bfloat16 [8, 256, 2, 2048], P('win', 'chan')
- window_gain: float32 [8], P('win'), may hold values from 0.4 to 3
- dead_mask: int32 [8, 256], P('win', 'chan'), may hold values 0 or 1
- order: int32 [256], replicated, may hold values from 0 to 15
Outputs:
- stack: bfloat16 [256, 256, 2, 2048], P(None, 'chan', None, 'win')
- window_weight: float32 [8], P('win')
The draws below stay inside these ranges and needn't reach their ends.
All inputs are finite; a program needn't handle non-finite values. No bound on the sum of `dead_mask` on one device may be relied on, other than what follows from the above.
Results may differ from the reference program's by a relative error of at most 0.0064.
Values may be sent and summed in bfloat16 or wider, within the bound.
A program may use at most 128 MiB of HBM per device.

```python
import math
import jax
import jax.numpy as jnp
from jax import lax

F = 2048
S = 256
ITERS = 2
C_DEV = 16
NW = 8
NCH = 256
SRC_DEV = 16


def draw_spectra(key, part):
    keys = jax.random.split(jax.random.fold_in(key, 11), 6)
    coherence = jax.random.uniform(keys[0], (NW, 1, 1, 1), jnp.float32, 0.2, 0.95)
    noise = jax.random.normal(keys[3], (NW, NCH, 2, F), jnp.float32)
    band_count = 32
    band_level = jnp.exp(jax.random.uniform(keys[4], (NW, band_count), jnp.float32, -2.5, 2.5))
    band_level = jnp.repeat(band_level, F // band_count, axis=1)
    block_count = NCH // C_DEV
    block_level = jnp.exp(jax.random.uniform(keys[5], (NW, block_count), jnp.float32, -1.5, 1.5))
    block_level = jnp.repeat(block_level, C_DEV, axis=1)
    noise = noise * band_level[:, None, None, :] * block_level[:, :, None, None]
    field = jax.random.normal(keys[1], (NW, 1, 2, F), jnp.float32)
    sensor = jax.random.normal(keys[2], (1, NCH, 2, F), jnp.float32)
    real_part = field[:, :, 0:1, :] * sensor[:, :, 0:1, :] - field[:, :, 1:2, :] * sensor[:, :, 1:2, :]
    imag_part = field[:, :, 0:1, :] * sensor[:, :, 1:2, :] + field[:, :, 1:2, :] * sensor[:, :, 0:1, :]
    common = jnp.concatenate([real_part, imag_part], axis=2) * 0.7071
    mixed = coherence * common + jnp.sqrt(1.0 - coherence * coherence) * noise
    chan_ramp = jnp.sqrt(1.0 + 2.0 * jnp.arange(NCH, dtype=jnp.float32) / NCH)
    freq_ramp = (1.0 + 2.0 * jnp.arange(F, dtype=jnp.float32) / F) ** 0.25
    mixed = mixed * chan_ramp[None, :, None, None] * freq_ramp[None, None, None, :]
    return mixed.astype(jnp.bfloat16)


def place_ends(drawn, key, smallest, high):
    place = [jax.random.randint(jax.random.fold_in(key, axis), (), 0, length) for axis, length in enumerate(drawn.shape)]
    main_axis = drawn.shape.index(max(drawn.shape))
    neighbour = place[:main_axis] + [(place[main_axis] + 1) % drawn.shape[main_axis]] + place[main_axis + 1:]
    return drawn.at[tuple(place)].set(smallest).at[tuple(neighbour)].set(high)


def shard_levels(key, dims, cuts, least, largest):
    loudness = 1.0
    for position, parts in cuts:
        heights = jax.random.uniform(jax.random.fold_in(jax.random.fold_in(key, 6), position), (parts,), jnp.float32, least / len(cuts), largest / len(cuts))
        loudness = loudness * jnp.repeat(jnp.exp(heights), dims[position] // parts).reshape((-1,) + (1,) * (len(dims) - 1 - position))
    return loudness


def setup_inputs(seed: int = 0) -> dict:
    seeds = jax.random.split(jax.random.key(seed), 5)
    spectra = draw_spectra(jax.random.fold_in(seeds[4], 71), 0)
    window_gain = jnp.clip(jnp.exp(math.log(3.0) - 2.014903 * jax.random.uniform(seeds[1], (NW,), jnp.float32) ** shard_levels(seeds[1], (NW,), ((0, 2),), -0.2, 0.2)), 0.4, 3.0)
    dead_mask = place_ends((jax.random.randint(seeds[2], (NW, NCH), 0, 8) < 7).astype(jnp.int32), jax.random.fold_in(seeds[2], 1), 0, 1)
    order = place_ends(jax.random.randint(seeds[3], (S,), 0, C_DEV), jax.random.fold_in(seeds[3], 1), 0, C_DEV - 1).astype(jnp.int32)
    return {"spectra": spectra, "window_gain": window_gain, "dead_mask": dead_mask, "order": order}


def reference(spectra, window_gain, dead_mask, order):
    f32 = jnp.float32
    bf16 = jnp.bfloat16
    scaled = (dead_mask.astype(f32)[:, :, None, None] * window_gain[:, None, None, None] * spectra.astype(f32)).astype(bf16)
    chosen = jnp.arange(S, dtype=jnp.int32) // SRC_DEV * C_DEV + order.astype(jnp.int32)
    source = jnp.take(scaled, chosen, axis=1)
    src_re = source[:, :, 0, :]
    src_im = source[:, :, 1, :]
    ch_re = scaled[:, :, 0, :]
    ch_im = scaled[:, :, 1, :]
    a_square = lax.optimization_barrier(jnp.sum(jnp.square(src_re.astype(f32)) + jnp.square(src_im.astype(f32)), axis=1))
    b_square = lax.optimization_barrier(jnp.sum(jnp.square(ch_re.astype(f32)) + jnp.square(ch_im.astype(f32)), axis=1))
    energy = lax.optimization_barrier(jnp.sum(a_square * b_square, axis=1))
    width = math.gcd(F, 64)
    blocks = F // width
    indices = jnp.arange(blocks, dtype=jnp.int32)

    def pieces(index):
        start = (index * width).astype(jnp.int32)
        return [lax.dynamic_slice_in_dim(v, start, width, 2).astype(f32) for v in (src_re, src_im, ch_re, ch_im)]

    def stack_block(weight, index):
        ar, ai, br, bi = pieces(index)
        total = jnp.sum(weight)
        wr = (weight[:, None, None] * br).astype(bf16)
        wi = (weight[:, None, None] * bi).astype(bf16)
        wr, wi = lax.optimization_barrier((wr, wi))
        wr = wr.astype(f32)
        wi = wi.astype(f32)
        gre = (jnp.einsum('ksf,kcf->scf', ar, wr) + jnp.einsum('ksf,kcf->scf', ai, wi)) / total
        gim = (jnp.einsum('ksf,kcf->scf', ar, wi) - jnp.einsum('ksf,kcf->scf', ai, wr)) / total
        return (gre.astype(bf16), gim.astype(bf16), ar, ai, br, bi)

    def misfit_block(weight, index):
        gre, gim, ar, ai, br, bi = stack_block(weight, index)
        gr = gre.astype(f32)
        gi = gim.astype(f32)
        p_re = jnp.einsum('ksf,scf->kcf', ar, gr) - jnp.einsum('ksf,scf->kcf', ai, gi)
        p_im = jnp.einsum('ksf,scf->kcf', ar, gi) + jnp.einsum('ksf,scf->kcf', ai, gr)
        cross = lax.optimization_barrier(jnp.sum(br * p_re + bi * p_im, axis=(1, 2)))
        power = jnp.sum(gr * gr + gi * gi)
        return (cross, power)
    weight = jnp.ones((NW,), f32)
    cells = S * NCH * F
    for step in range(ITERS):
        crosses, powers = lax.map(lambda index: misfit_block(weight, index), indices)
        misfit = energy - 2.0 * lax.optimization_barrier(jnp.sum(crosses, axis=0)) + jnp.sum(powers)
        weight = 1.0 / jnp.sqrt(misfit / cells + 1e-06)
    gre, gim = lax.map(lambda index: stack_block(weight, index)[:2], indices)
    joined = jnp.stack([gre, gim], axis=1)
    stack = jnp.transpose(joined, (2, 3, 1, 0, 4)).reshape(S, NCH, 2, F)
    window_weight = weight * (NW / jnp.sum(weight))
    return (stack, window_weight)
```

```python
import functools

import jax
import jax.numpy as jnp
from jax import lax
from jax.experimental import pallas as pl
from jax.experimental.pallas import tpu as pltpu
from jax.sharding import PartitionSpec as P

ITERS = 2
LANES = 128
PART = 4
MESH = pl.DeviceIdType.MESH


def solve_stack(src_re, src_im, ch_re, ch_im, cells):
    f32 = jnp.float32
    bf16 = jnp.bfloat16
    corr_form = "ksf,kcf->scf"
    proj_form = "ksf,scf->kcf"
    row_axis = 1
    freq_axis = 1
    cross_axes = (1, 2)
    count = src_re.shape[0]
    a_square = jnp.sum(
        jnp.square(src_re.astype(f32)) + jnp.square(src_im.astype(f32)), axis=row_axis
    )
    b_square = jnp.sum(jnp.square(ch_re.astype(f32)) + jnp.square(ch_im.astype(f32)), axis=row_axis)
    energy = jnp.sum(a_square * b_square, axis=freq_axis)

    def product(form, left, right):
        return jnp.einsum(form, left, right, preferred_element_type=f32)

    def stack_of(weight):
        shaped = weight[:, None, None]
        w_re = (shaped * ch_re.astype(f32)).astype(bf16)
        w_im = (shaped * ch_im.astype(f32)).astype(bf16)
        total = jnp.sum(weight)
        gre = (product(corr_form, src_re, w_re) + product(corr_form, src_im, w_im)) / total
        gim = (product(corr_form, src_re, w_im) - product(corr_form, src_im, w_re)) / total
        return (gre.astype(bf16), gim.astype(bf16))

    weight = jnp.ones((count,), f32)
    for step in range(ITERS):
        gre, gim = stack_of(weight)
        p_re = product(proj_form, src_re, gre) - product(proj_form, src_im, gim)
        p_im = product(proj_form, src_re, gim) + product(proj_form, src_im, gre)
        cross = jnp.sum(ch_re.astype(f32) * p_re + ch_im.astype(f32) * p_im, axis=cross_axes)
        power = jnp.sum(jnp.square(gre.astype(f32)) + jnp.square(gim.astype(f32)))
        partial_misfit = energy - 2.0 * cross + power
        misfit = lax.psum(partial_misfit, ("win", "chan"))
        weight = 1.0 / jnp.sqrt(misfit / cells + 1e-06)
    gre, gim = stack_of(weight)
    return (gre, gim, weight)


def body(spectra, window_gain, dead_mask, order):
    f32 = jnp.float32
    bf16 = jnp.bfloat16
    scaled = (
        dead_mask.astype(f32)[:, :, None, None]
        * window_gain[:, None, None, None]
        * spectra.astype(f32)
    ).astype(bf16)
    sources = order.shape[0]
    per_dev = sources // lax.axis_size("chan")
    channels = spectra.shape[1]
    cells = sources * channels * lax.axis_size("chan") * spectra.shape[3]
    local = lax.all_to_all(scaled, "win", split_axis=3, concat_axis=0, tiled=True)
    first = lax.axis_index("chan") * per_dev
    mine = lax.dynamic_slice_in_dim(order, first, per_dev, 0)
    picked = jnp.take(local, mine, axis=1)
    gathered = lax.all_gather(picked, "chan", axis=1, tiled=True)
    gre, gim, weight = solve_stack(
        gathered[:, :, 0, :], gathered[:, :, 1, :], local[:, :, 0, :], local[:, :, 1, :], cells
    )
    stack = jnp.stack([gre, gim], axis=2)
    count = weight.shape[0]
    normed = weight * (count / jnp.sum(weight))
    first_window = lax.axis_index("win") * spectra.shape[0]
    window_weight = lax.dynamic_slice_in_dim(normed, first_window, spectra.shape[0], 0)
    return (stack, window_weight)


def even_rows(shape):
    return lax.rem(lax.broadcasted_iota(jnp.int32, shape, len(shape) - 2), 2) == 0


def next_row(x):
    return pltpu.roll(x, x.shape[0] - 1, 0)


def prev_row(x):
    return pltpu.roll(x, 1, 0)


def swapped(x, even):
    return jnp.where(even, next_row(x), prev_row(x))


def gather_kernel(
    cells,
    scale_ref,
    count_ref,
    spectra_ref,
    out_ref,
    weight_ref,
    held,
    away,
    grams,
    lines,
    sums,
    halves,
    out_sem,
    x_sems,
    up_sems,
    down_sems,
    y_sems,
    pair_sems,
    sum_sems,
    half_sems,
):
    f32 = jnp.float32
    bf16 = jnp.bfloat16
    total = lax.axis_size("chan")
    depth = total // 4
    me = lax.axis_index("chan")
    win = lax.axis_index("win")
    core = lax.rem(me, 2)
    row = lax.rem(me // 2, 2)
    level = me // 4
    windows, channels, rows = held.shape[1], held.shape[2], held.shape[3]
    mine = windows // 2
    step_windows = windows // PART
    other = {"win": 1 - win}

    def place(z, y):
        return (z * 2 + y) * 2 + core

    barrier = pltpu.get_barrier_semaphore()

    @pl.loop(1, total)
    def _(i):
        pl.semaphore_signal(
            barrier, inc=1, device_id={"chan": lax.rem(me + i, total)}, device_id_type=MESH
        )

    pl.semaphore_signal(barrier, inc=1, device_id=other, device_id_type=MESH)

    for half in range(2):

        @pl.when(win == half)
        def _():
            for k in range(mine):

                @pl.loop(0, channels)
                def _(c):
                    scale = scale_ref[k, c]
                    for part in range(2):
                        value = spectra_ref[k, c, part * rows : (part + 1) * rows, :].astype(f32)
                        value = (scale * value).astype(bf16)
                        if part == half:
                            held[me, half * mine + k, c] = value
                        else:
                            away[k, c] = value

    pl.semaphore_wait(barrier, total)

    def across(j):
        start = pl.ds(j * step_windows, step_windows)
        return pltpu.make_async_remote_copy(
            src_ref=away.at[start],
            dst_ref=held.at[me, pl.ds(win * mine + j * step_windows, step_windows)],
            send_sem=x_sems.at[0, j],
            recv_sem=x_sems.at[1, j],
            device_id=other,
            device_id_type=MESH,
        )

    for j in range(PART // 2):
        across(j).start()

    def piece(block, q):
        return held.at[block, pl.ds(q * step_windows, step_windows)]

    def send(block, q, sems, slot_out, slot_in, target):
        return pltpu.make_async_remote_copy(
            src_ref=piece(block, q),
            dst_ref=piece(block, q),
            send_sem=sems.at[0, slot_out, q],
            recv_sem=sems.at[1, slot_in, q],
            device_id={"chan": target},
            device_id_type=MESH,
        )

    sibling = me + 1 - 2 * core

    def up(block, q, t):
        return send(block, q, up_sems, t, t + 1, lax.rem(me + 4, total))

    def down(block, q, t):
        return send(block, q, down_sems, t, t + 1, lax.rem(me + total - 4, total))

    def cross(z, q):
        return send(place(z, row), q, y_sems, z, z, place(level, 1 - row))

    def pair(block, q):
        return send(block, q, pair_sems, block // 2, block // 2, sibling)

    def arrive(block, q, sems, slot):
        send(block, q, sems, slot, slot, sibling).wait_recv()

    def each(t, act):
        if t == 0:
            act(level, True, True)
        else:

            @pl.when(level - t >= 0)
            def _():
                act(level - t, True, False)

            @pl.when(level + t < depth)
            def _():
                act(level + t, False, True)

    def spread(t, q, act):
        def one(z, rising, falling):
            block = place(z, row)
            if t > 0:
                if act == "start":
                    arrive(block, q, up_sems if rising else down_sems, t)
            run = lambda copy: copy.start() if act == "start" else copy.wait_send()
            if rising and t < depth - 1:

                @pl.when(level < depth - 1)
                def _():
                    run(up(block, q, t))

            if falling and t < depth - 1:

                @pl.when(level > 0)
                def _():
                    run(down(block, q, t))

            run(cross(z, q))
            run(pair(block, q))

        each(t, one)

    def receive_cross(t, q, act):
        def one(z, rising, falling):
            block = place(z, 1 - row)
            if act == "start":
                arrive(block, q, y_sems, z)
                pair(block, q).start()
            else:
                pair(block, q).wait_send()

        each(t, one)

    for t in range(depth + 1):

        @pl.loop(0, PART)
        def _(p):
            q = lax.rem(p + win * (PART // 2), PART)
            if t == 0:

                @pl.when(p >= PART // 2)
                def _():
                    across(p - PART // 2).wait_recv()

            if t < depth:
                spread(t, q, "start")
            if t > 0:
                receive_cross(t - 1, q, "start")

    @pl.loop(0, total // 2)
    def _(i):
        @pl.loop(0, PART)
        def _(q):
            block = i * 2 + 1 - core
            arrive(block, q, pair_sems, i)

    copy_out = pltpu.make_async_copy(held, out_ref, out_sem)
    copy_out.start()

    even = even_rows((rows, LANES))
    for k in range(windows):
        for j in range(k, windows):
            for form in range(2):
                grams[0, form, k * windows + j] = jnp.zeros((rows, LANES), f32)
                grams[1, form, k * windows + j] = jnp.zeros((rows, LANES), f32)

    @pl.loop(0, total + 1)
    def _(i):
        block = jnp.where(i == total, me, i)
        which = jnp.where(i == total, 1, 0)
        for k in range(windows):
            zero = jnp.zeros((rows, LANES), f32)

            def add(c, carry):
                plain, turned = carry
                x = held[block, k, c].astype(f32) * count_ref[i, c]
                y = swapped(x, even)
                new_plain, new_turned = [], []
                for j in range(k, windows):
                    z = held[block, j, c].astype(f32)
                    new_plain.append(plain[j - k] + x * z)
                    new_turned.append(turned[j - k] + y * z)
                return tuple(new_plain), tuple(new_turned)

            span = (zero,) * (windows - k)
            plain, turned = lax.fori_loop(0, channels, add, (span, span))
            for j in range(k, windows):
                grams[which, 0, k * windows + j] += plain[j - k]
                grams[which, 1, k * windows + j] += turned[j - k]

    for k in range(windows):
        for j in range(k, windows):
            at = k * windows + j
            value = jnp.zeros((rows, LANES), f32)
            for form in range(2):
                a, b = grams[0, form, at], grams[1, form, at]
                sign = 1.0 if form == 0 else -1.0
                value += (a + sign * next_row(a)) * (b + sign * next_row(b))
            line = jnp.sum(jnp.where(even, value, 0.0), axis=0, keepdims=True)
            lines[k, j : j + 1, :] = line
            lines[j, k : k + 1, :] = line

    lane = lax.broadcasted_iota(jnp.int32, (windows, LANES), 1)
    sub = lax.broadcasted_iota(jnp.int32, (windows, LANES), 0)
    part = jnp.zeros((windows, LANES), f32)
    for k in range(windows):
        part = jnp.where(lane == k, jnp.sum(lines[k], axis=1, keepdims=True), part)
    sums[me] = part

    def share(i):
        target = lax.rem(me + i, total)
        return pltpu.make_async_remote_copy(
            src_ref=sums.at[me],
            dst_ref=sums.at[me],
            send_sem=sum_sems.at[0, target],
            recv_sem=sum_sems.at[1, me],
            device_id={"chan": target},
            device_id_type=MESH,
        )

    @pl.loop(1, total)
    def _(i):
        share(i).start()

    @pl.loop(1, total)
    def _(i):
        source = lax.rem(me + i, total)
        pltpu.make_async_remote_copy(
            src_ref=sums.at[source],
            dst_ref=sums.at[source],
            send_sem=sum_sems.at[0, source],
            recv_sem=sum_sems.at[1, source],
            device_id={"chan": source},
            device_id_type=MESH,
        ).wait_recv()

    group = sums[0]
    for i in range(1, total):
        group = group + sums[i]
    halves[0] = group
    trade = pltpu.make_async_remote_copy(
        src_ref=halves.at[0],
        dst_ref=halves.at[1],
        send_sem=half_sems.at[0],
        recv_sem=half_sems.at[1],
        device_id=other,
        device_id_type=MESH,
    )
    trade.start()
    trade.wait_recv()
    table = halves[0] + halves[1]
    diagonal = lane == sub
    energy = jnp.sum(jnp.where(diagonal, table, 0.0), axis=0, keepdims=True)
    live = lane[:1] < windows
    weight = jnp.where(live, 1.0, 0.0)
    for _ in range(ITERS):
        column = jnp.sum(jnp.where(diagonal, weight, 0.0), axis=1, keepdims=True)
        total_weight = jnp.sum(weight, axis=1, keepdims=True)
        cross_row = jnp.sum(table * column, axis=0, keepdims=True) / total_weight
        power = jnp.sum(weight * cross_row, axis=1, keepdims=True) / total_weight
        misfit = energy - 2.0 * cross_row + power
        weight = jnp.where(live, 1.0 / jnp.sqrt(misfit / cells + 1e-06), 0.0)
    weight_ref[...] = weight / jnp.sum(weight, axis=1, keepdims=True)

    for j in range(PART // 2):
        across(j).wait_send()
    for t in range(depth + 1):

        @pl.loop(0, PART)
        def _(q):
            if t < depth:
                spread(t, q, "end")
            if t > 0:
                receive_cross(t - 1, q, "end")

    @pl.loop(1, total)
    def _(i):
        share(i).wait_send()

    trade.wait_send()
    copy_out.wait()


def stack_kernel(pick_ref, weight_ref, source_ref, own_ref, out_ref, turned, first, second):
    f32 = jnp.float32
    bf16 = jnp.bfloat16
    windows, channels, rows = turned.shape[0], turned.shape[1], turned.shape[2]
    step = pl.program_id(0)
    even = even_rows((rows, LANES))
    per = out_ref.shape[0]

    @pl.when(step == 0)
    def _():
        for k in range(windows):

            @pl.loop(0, channels)
            def _(c):
                x = own_ref[0, k, c].astype(f32) * weight_ref[0, k]
                first[c, k] = jnp.where(even, x, -prev_row(x)).astype(bf16)
                second[c, k] = jnp.where(even, next_row(x), x).astype(bf16)

    for k in range(windows):

        @pl.loop(0, channels, unroll=4)
        def _(c):
            x = source_ref[0, k, c].astype(f32)
            turned[k, c] = swapped(x, even).astype(bf16)

    @pl.loop(0, per // 2)
    def _(pair):
        base = step * per + pair * 2
        chosen = [pick_ref[base], pick_ref[base + 1]]
        a = [[source_ref[0, k, i] for k in range(windows)] for i in chosen]
        t = [[turned[k, i] for k in range(windows)] for i in chosen]

        @pl.loop(0, channels, unroll=2)
        def _(c):
            b = [first[c, k] for k in range(windows)]
            d = [second[c, k] for k in range(windows)]
            for u in range(2):
                terms = [a[u][k] * b[k] + t[u][k] * d[k] for k in range(windows)]
                while len(terms) > 1:
                    terms = [terms[i] + terms[i + 1] for i in range(0, len(terms), 2)]
                out_ref[pair * 2 + u, c] = terms[0]


def tiled(x):
    lead, bins = x.shape[:-2], x.shape[-1]
    x = x.reshape(*lead, 2, bins // LANES, LANES)
    return jnp.swapaxes(x, -3, -2).reshape(*lead, bins // LANES * 2, LANES)


def fast_body(spectra, window_gain, dead_mask, order):
    f32 = jnp.float32
    bf16 = jnp.bfloat16
    total = lax.axis_size("chan")
    mine, channels, _, bins = spectra.shape
    windows = mine * 2
    rows = bins // LANES
    sources = order.shape[0]
    per = sources // total
    cells = float(sources * channels * total * bins)
    scale = dead_mask.astype(f32) * window_gain[:, None]
    hits = order.reshape(total, per, 1) == jnp.arange(channels, dtype=jnp.int32)
    count = jnp.sum(hits.astype(f32), axis=1)
    count = jnp.concatenate([count, jnp.ones((1, channels), f32)], axis=0)
    smem = pl.BlockSpec(memory_space=pltpu.SMEM)
    vmem = pl.BlockSpec(memory_space=pltpu.VMEM)
    dma = pltpu.SemaphoreType.DMA
    depth = total // 4
    gathered, weight = pl.pallas_call(
        functools.partial(gather_kernel, cells),
        out_shape=(
            jax.ShapeDtypeStruct((total, windows, channels, rows, LANES), bf16),
            jax.ShapeDtypeStruct((1, LANES), f32),
        ),
        in_specs=[smem, smem, vmem],
        out_specs=(pl.BlockSpec(memory_space=pl.ANY), vmem),
        scratch_shapes=[
            pltpu.VMEM((total, windows, channels, rows, LANES), bf16),
            pltpu.VMEM((mine, channels, rows, LANES), bf16),
            pltpu.VMEM((2, 2, windows * windows, rows, LANES), f32),
            pltpu.VMEM((windows, windows, LANES), f32),
            pltpu.VMEM((total, windows, LANES), f32),
            pltpu.VMEM((2, windows, LANES), f32),
            dma,
            dma((2, PART // 2)),
            dma((2, depth + 1, PART)),
            dma((2, depth + 1, PART)),
            dma((2, depth, PART)),
            dma((2, total // 2, PART)),
            dma((2, total)),
            dma((2,)),
        ],
        compiler_params=pltpu.CompilerParams(
            collective_id=0, has_side_effects=True, vmem_limit_bytes=40 * 2**20
        ),
        name="gather_sources",
    )(scale, count, tiled(spectra))
    pick = jnp.concatenate([order, lax.axis_index("chan")[None].astype(jnp.int32)])
    block = (1, windows, channels, rows, LANES)
    stack = pl.pallas_call(
        stack_kernel,
        out_shape=jax.ShapeDtypeStruct((sources, channels, rows, LANES), bf16),
        grid_spec=pltpu.PrefetchScalarGridSpec(
            num_scalar_prefetch=1,
            grid=(total,),
            in_specs=[
                smem,
                pl.BlockSpec(block, lambda i, pick: (i, 0, 0, 0, 0)),
                pl.BlockSpec(block, lambda i, pick: (pick[sources], 0, 0, 0, 0)),
            ],
            out_specs=pl.BlockSpec((per, channels, rows, LANES), lambda i, pick: (i, 0, 0, 0)),
            scratch_shapes=[
                pltpu.VMEM((windows, channels, rows, LANES), bf16),
                pltpu.VMEM((channels, windows, rows, LANES), bf16),
                pltpu.VMEM((channels, windows, rows, LANES), bf16),
            ],
        ),
        compiler_params=pltpu.CompilerParams(vmem_limit_bytes=40 * 2**20),
        name="stack_sources",
    )(pick, weight, gathered, gathered)
    stack = stack.reshape(sources, channels, rows // 2, 2, LANES)
    stack = jnp.swapaxes(stack, 2, 3).reshape(sources, channels, 2, bins // 2)
    first = lax.axis_index("win") * mine
    window_weight = windows * lax.dynamic_slice_in_dim(weight[0], first, mine, 0)
    return (stack, window_weight)


def solution(mesh):
    placed = (P("win", "chan", None, None), P("win"), P("win", "chan"), P())
    wins, chans = mesh.shape["win"], mesh.shape["chan"]

    def chosen(spectra, window_gain, dead_mask, order):
        windows, _, _, bins = spectra.shape
        fits = wins == 2 and windows * wins == 8 and chans % 4 == 0
        fits = fits and bins % (16 * LANES) == 0 and order.shape[0] % (2 * chans) == 0
        return (fast_body if fits else body)(spectra, window_gain, dead_mask, order)

    return jax.shard_map(
        chosen,
        mesh=mesh,
        in_specs=placed,
        out_specs=(P(None, "chan", None, "win"), P("win")),
        check_vma=False,
    )
```

```python
import functools

import jax
import jax.numpy as jnp
from jax import lax
from jax.experimental import pallas as pl
from jax.experimental.pallas import tpu as pltpu
from jax.sharding import PartitionSpec as P

ITERS = 2
LANES = 128
PART = 4
MESH = pl.DeviceIdType.MESH


def solve_stack(src_re, src_im, ch_re, ch_im, cells):
    f32 = jnp.float32
    bf16 = jnp.bfloat16
    corr_form = "ksf,kcf->scf"
    proj_form = "ksf,scf->kcf"
    row_axis = 1
    freq_axis = 1
    cross_axes = (1, 2)
    count = src_re.shape[0]
    a_square = jnp.sum(
        jnp.square(src_re.astype(f32)) + jnp.square(src_im.astype(f32)), axis=row_axis
    )
    b_square = jnp.sum(jnp.square(ch_re.astype(f32)) + jnp.square(ch_im.astype(f32)), axis=row_axis)
    energy = jnp.sum(a_square * b_square, axis=freq_axis)

    def product(form, left, right):
        return jnp.einsum(form, left, right, preferred_element_type=f32)

    def stack_of(weight):
        shaped = weight[:, None, None]
        w_re = (shaped * ch_re.astype(f32)).astype(bf16)
        w_im = (shaped * ch_im.astype(f32)).astype(bf16)
        total = jnp.sum(weight)
        gre = (product(corr_form, src_re, w_re) + product(corr_form, src_im, w_im)) / total
        gim = (product(corr_form, src_re, w_im) - product(corr_form, src_im, w_re)) / total
        return (gre.astype(bf16), gim.astype(bf16))

    weight = jnp.ones((count,), f32)
    for step in range(ITERS):
        gre, gim = stack_of(weight)
        p_re = product(proj_form, src_re, gre) - product(proj_form, src_im, gim)
        p_im = product(proj_form, src_re, gim) + product(proj_form, src_im, gre)
        cross = jnp.sum(ch_re.astype(f32) * p_re + ch_im.astype(f32) * p_im, axis=cross_axes)
        power = jnp.sum(jnp.square(gre.astype(f32)) + jnp.square(gim.astype(f32)))
        partial_misfit = energy - 2.0 * cross + power
        misfit = lax.psum(partial_misfit, ("win", "chan"))
        weight = 1.0 / jnp.sqrt(misfit / cells + 1e-06)
    gre, gim = stack_of(weight)
    return (gre, gim, weight)


def body(spectra, window_gain, dead_mask, order):
    f32 = jnp.float32
    bf16 = jnp.bfloat16
    scaled = (
        dead_mask.astype(f32)[:, :, None, None]
        * window_gain[:, None, None, None]
        * spectra.astype(f32)
    ).astype(bf16)
    sources = order.shape[0]
    per_dev = sources // lax.axis_size("chan")
    channels = spectra.shape[1]
    cells = sources * channels * lax.axis_size("chan") * spectra.shape[3]
    local = lax.all_to_all(scaled, "win", split_axis=3, concat_axis=0, tiled=True)
    first = lax.axis_index("chan") * per_dev
    mine = lax.dynamic_slice_in_dim(order, first, per_dev, 0)
    picked = jnp.take(local, mine, axis=1)
    gathered = lax.all_gather(picked, "chan", axis=1, tiled=True)
    gre, gim, weight = solve_stack(
        gathered[:, :, 0, :], gathered[:, :, 1, :], local[:, :, 0, :], local[:, :, 1, :], cells
    )
    stack = jnp.stack([gre, gim], axis=2)
    count = weight.shape[0]
    normed = weight * (count / jnp.sum(weight))
    first_window = lax.axis_index("win") * spectra.shape[0]
    window_weight = lax.dynamic_slice_in_dim(normed, first_window, spectra.shape[0], 0)
    return (stack, window_weight)


def even_rows(shape):
    return lax.rem(lax.broadcasted_iota(jnp.int32, shape, len(shape) - 2), 2) == 0


def next_row(x):
    return pltpu.roll(x, x.shape[0] - 1, 0)


def prev_row(x):
    return pltpu.roll(x, 1, 0)


def swapped(x, even):
    return jnp.where(even, next_row(x), prev_row(x))


def gather_kernel(
    cells,
    scale_ref,
    count_ref,
    spectra_ref,
    out_ref,
    weight_ref,
    held,
    away,
    grams,
    lines,
    sums,
    halves,
    out_sems,
    x_sems,
    up_sems,
    down_sems,
    y_sems,
    pair_sems,
    sum_sems,
    half_sems,
):
    f32 = jnp.float32
    bf16 = jnp.bfloat16
    total = lax.axis_size("chan")
    depth = total // 4
    me = lax.axis_index("chan")
    win = lax.axis_index("win")
    core = lax.rem(me, 2)
    row = lax.rem(me // 2, 2)
    level = me // 4
    windows, channels, rows = held.shape[1], held.shape[2], held.shape[3]
    mine = windows // 2
    step_windows = windows // PART
    other = {"win": 1 - win}

    def place(z, y):
        return (z * 2 + y) * 2 + core

    barrier = pltpu.get_barrier_semaphore()

    @pl.loop(1, total)
    def _(i):
        pl.semaphore_signal(
            barrier, inc=1, device_id={"chan": lax.rem(me + i, total)}, device_id_type=MESH
        )

    pl.semaphore_signal(barrier, inc=1, device_id=other, device_id_type=MESH)

    for half in range(2):

        @pl.when(win == half)
        def _():
            for k in range(mine):

                @pl.loop(0, channels)
                def _(c):
                    scale = scale_ref[k, c]
                    for part in range(2):
                        value = spectra_ref[k, c, part * rows : (part + 1) * rows, :].astype(f32)
                        value = (scale * value).astype(bf16)
                        if part == half:
                            held[me, half * mine + k, c] = value
                        else:
                            away[k, c] = value

    pl.semaphore_wait(barrier, total)

    def across(j):
        start = pl.ds(j * step_windows, step_windows)
        return pltpu.make_async_remote_copy(
            src_ref=away.at[start],
            dst_ref=held.at[me, pl.ds(win * mine + j * step_windows, step_windows)],
            send_sem=x_sems.at[0, j],
            recv_sem=x_sems.at[1, j],
            device_id=other,
            device_id_type=MESH,
        )

    for j in range(PART // 2):
        across(j).start()

    def piece(block, q):
        return held.at[block, pl.ds(q * step_windows, step_windows)]

    def send(block, q, sems, slot_out, slot_in, target):
        return pltpu.make_async_remote_copy(
            src_ref=piece(block, q),
            dst_ref=piece(block, q),
            send_sem=sems.at[0, slot_out, q],
            recv_sem=sems.at[1, slot_in, q],
            device_id={"chan": target},
            device_id_type=MESH,
        )

    sibling = me + 1 - 2 * core

    def up(block, q, t):
        return send(block, q, up_sems, t, t + 1, lax.rem(me + 4, total))

    def down(block, q, t):
        return send(block, q, down_sems, t, t + 1, lax.rem(me + total - 4, total))

    def cross(z, q):
        return send(place(z, row), q, y_sems, z, z, place(level, 1 - row))

    def pair(block, q):
        return send(block, q, pair_sems, block // 2, block // 2, sibling)

    def arrive(block, q, sems, slot):
        send(block, q, sems, slot, slot, sibling).wait_recv()

    def each(t, act):
        if t == 0:
            act(level, True, True)
        else:

            @pl.when(level - t >= 0)
            def _():
                act(level - t, True, False)

            @pl.when(level + t < depth)
            def _():
                act(level + t, False, True)

    def spread(t, q, act):
        def one(z, rising, falling):
            block = place(z, row)
            if t > 0:
                if act == "start":
                    arrive(block, q, up_sems if rising else down_sems, t)
            run = lambda copy: copy.start() if act == "start" else copy.wait_send()
            if rising and t < depth - 1:

                @pl.when(level < depth - 1)
                def _():
                    run(up(block, q, t))

            if falling and t < depth - 1:

                @pl.when(level > 0)
                def _():
                    run(down(block, q, t))

            run(cross(z, q))
            run(pair(block, q))

        each(t, one)

    def receive_cross(t, q, act):
        def one(z, rising, falling):
            block = place(z, 1 - row)
            if act == "start":
                arrive(block, q, y_sems, z)
                pair(block, q).start()
            else:
                pair(block, q).wait_send()

        each(t, one)

    even = even_rows((rows, LANES))
    for k in range(windows):
        for j in range(k, windows):
            for form in range(2):
                grams[0, form, k * windows + j] = jnp.zeros((rows, LANES), f32)
                grams[1, form, k * windows + j] = jnp.zeros((rows, LANES), f32)

    def gram(which, block, factors):
        for k in range(windows):
            zero = jnp.zeros((rows, LANES), f32)

            def add(c, carry):
                plain, turned = carry
                x = held[block, k, c].astype(f32) * count_ref[factors, c]
                y = swapped(x, even)
                new_plain, new_turned = [], []
                for j in range(k, windows):
                    z = held[block, j, c].astype(f32)
                    new_plain.append(plain[j - k] + x * z)
                    if j > k:
                        new_turned.append(turned[j - k - 1] + y * z)
                return tuple(new_plain), tuple(new_turned)

            span = (zero,) * (windows - k)
            plain, turned = lax.fori_loop(0, channels, add, (span, span[1:]), unroll=4)
            for j in range(k, windows):
                grams[which, 0, k * windows + j] += plain[j - k]
                if j > k:
                    grams[which, 1, k * windows + j] += turned[j - k - 1]

    def copy_out(block):
        return pltpu.make_async_copy(held.at[block], out_ref.at[block], out_sems.at[block])

    def settle(t, y, theirs):
        def one(z, rising, falling):
            mate = place(z, y)
            block = mate + theirs * (1 - 2 * core)

            @pl.when(theirs == 1)
            def _():
                for q in range(PART):
                    arrive(block, q, pair_sems, block // 2)

            copy_out(block).start()
            gram(0, block, block)

        if t >= 0:
            each(t, one)

    for t in range(depth + 1):

        @pl.loop(0, PART)
        def _(p):
            q = lax.rem(p + win * (PART // 2), PART)
            if t == 0:

                @pl.when(p >= PART // 2)
                def _():
                    across(p - PART // 2).wait_recv()

            if t < depth:
                spread(t, q, "start")
            if t > 0:
                receive_cross(t - 1, q, "start")

                @pl.when(p < 2)
                def _():
                    settle(t - 1, row, p)

                @pl.when(p >= 2)
                def _():
                    settle(t - 2, 1 - row, p - 2)

        if t == 0:
            gram(1, me, total)

    @pl.loop(0, 2)
    def _(p):
        settle(depth - 1, 1 - row, p)

    for k in range(windows):
        for j in range(k, windows):
            at = k * windows + j
            value = jnp.zeros((rows, LANES), f32)
            for form in range(2):
                a, b = grams[0, form, at], grams[1, form, at]
                sign = 1.0 if form == 0 else -1.0
                value += (a + sign * next_row(a)) * (b + sign * next_row(b))
            line = jnp.sum(jnp.where(even, value, 0.0), axis=0, keepdims=True)
            lines[k, j : j + 1, :] = line
            lines[j, k : k + 1, :] = line

    lane = lax.broadcasted_iota(jnp.int32, (windows, LANES), 1)
    sub = lax.broadcasted_iota(jnp.int32, (windows, LANES), 0)
    part = jnp.zeros((windows, LANES), f32)
    for k in range(windows):
        part = jnp.where(lane == k, jnp.sum(lines[k], axis=1, keepdims=True), part)
    sums[me] = part

    def share(i):
        target = lax.rem(me + i, total)
        return pltpu.make_async_remote_copy(
            src_ref=sums.at[me],
            dst_ref=sums.at[me],
            send_sem=sum_sems.at[0, target],
            recv_sem=sum_sems.at[1, me],
            device_id={"chan": target},
            device_id_type=MESH,
        )

    @pl.loop(1, total)
    def _(i):
        share(i).start()

    @pl.loop(1, total)
    def _(i):
        source = lax.rem(me + i, total)
        pltpu.make_async_remote_copy(
            src_ref=sums.at[source],
            dst_ref=sums.at[source],
            send_sem=sum_sems.at[0, source],
            recv_sem=sum_sems.at[1, source],
            device_id={"chan": source},
            device_id_type=MESH,
        ).wait_recv()

    group = sums[0]
    for i in range(1, total):
        group = group + sums[i]
    halves[0] = group
    trade = pltpu.make_async_remote_copy(
        src_ref=halves.at[0],
        dst_ref=halves.at[1],
        send_sem=half_sems.at[0],
        recv_sem=half_sems.at[1],
        device_id=other,
        device_id_type=MESH,
    )
    trade.start()
    trade.wait_recv()
    table = halves[0] + halves[1]
    diagonal = lane == sub
    energy = jnp.sum(jnp.where(diagonal, table, 0.0), axis=0, keepdims=True)
    live = lane[:1] < windows
    weight = jnp.where(live, 1.0, 0.0)
    for _ in range(ITERS):
        column = jnp.sum(jnp.where(diagonal, weight, 0.0), axis=1, keepdims=True)
        total_weight = jnp.sum(weight, axis=1, keepdims=True)
        cross_row = jnp.sum(table * column, axis=0, keepdims=True) / total_weight
        power = jnp.sum(weight * cross_row, axis=1, keepdims=True) / total_weight
        misfit = energy - 2.0 * cross_row + power
        weight = jnp.where(live, 1.0 / jnp.sqrt(misfit / cells + 1e-06), 0.0)
    weight_ref[...] = weight / jnp.sum(weight, axis=1, keepdims=True)

    for j in range(PART // 2):
        across(j).wait_send()
    for t in range(depth + 1):

        @pl.loop(0, PART)
        def _(q):
            if t < depth:
                spread(t, q, "end")
            if t > 0:
                receive_cross(t - 1, q, "end")

    @pl.loop(1, total)
    def _(i):
        share(i).wait_send()

    trade.wait_send()

    @pl.loop(0, total)
    def _(i):
        copy_out(i).wait()


def stack_kernel(pick_ref, weight_ref, source_ref, own_ref, out_ref, turned, first, second):
    f32 = jnp.float32
    bf16 = jnp.bfloat16
    windows, channels, rows = turned.shape[0], turned.shape[1], turned.shape[2]
    step = pl.program_id(0)
    even = even_rows((rows, LANES))
    per = out_ref.shape[0]

    @pl.when(step == 0)
    def _():
        for k in range(windows):

            @pl.loop(0, channels)
            def _(c):
                x = own_ref[0, k, c].astype(f32) * weight_ref[0, k]
                x = x.astype(bf16).astype(f32)
                first[c, k] = jnp.where(even, x, -prev_row(x))
                second[c, k] = jnp.where(even, next_row(x), x)

    for k in range(windows):

        @pl.loop(0, channels, unroll=4)
        def _(c):
            x = source_ref[0, k, c].astype(f32)
            turned[k, c] = swapped(x, even).astype(bf16)

    @pl.loop(0, per)
    def _(s):
        i = pick_ref[step * per + s]
        a = [source_ref[0, k, i].astype(f32) for k in range(windows)]
        t = [turned[k, i].astype(f32) for k in range(windows)]

        @pl.loop(0, channels, unroll=16)
        def _(c):
            value = None
            for k in range(windows):
                term = a[k] * first[c, k] + t[k] * second[c, k]
                value = term if value is None else value + term
            out_ref[s, c] = value.astype(bf16)


def tiled(x):
    lead, bins = x.shape[:-2], x.shape[-1]
    x = x.reshape(*lead, 2, bins // LANES, LANES)
    return jnp.swapaxes(x, -3, -2).reshape(*lead, bins // LANES * 2, LANES)


def fast_body(spectra, window_gain, dead_mask, order):
    f32 = jnp.float32
    bf16 = jnp.bfloat16
    total = lax.axis_size("chan")
    mine, channels, _, bins = spectra.shape
    windows = mine * 2
    rows = bins // LANES
    sources = order.shape[0]
    per = sources // total
    cells = float(sources * channels * total * bins)
    scale = dead_mask.astype(f32) * window_gain[:, None]
    hits = order.reshape(total, per, 1) == jnp.arange(channels, dtype=jnp.int32)
    count = jnp.sum(hits.astype(f32), axis=1)
    count = jnp.concatenate([count, jnp.ones((1, channels), f32)], axis=0)
    smem = pl.BlockSpec(memory_space=pltpu.SMEM)
    vmem = pl.BlockSpec(memory_space=pltpu.VMEM)
    dma = pltpu.SemaphoreType.DMA
    depth = total // 4
    gathered, weight = pl.pallas_call(
        functools.partial(gather_kernel, cells),
        out_shape=(
            jax.ShapeDtypeStruct((total, windows, channels, rows, LANES), bf16),
            jax.ShapeDtypeStruct((1, LANES), f32),
        ),
        in_specs=[smem, smem, vmem],
        out_specs=(pl.BlockSpec(memory_space=pl.ANY), vmem),
        scratch_shapes=[
            pltpu.VMEM((total, windows, channels, rows, LANES), bf16),
            pltpu.VMEM((mine, channels, rows, LANES), bf16),
            pltpu.VMEM((2, 2, windows * windows, rows, LANES), f32),
            pltpu.VMEM((windows, windows, LANES), f32),
            pltpu.VMEM((total, windows, LANES), f32),
            pltpu.VMEM((2, windows, LANES), f32),
            dma((total,)),
            dma((2, PART // 2)),
            dma((2, depth + 1, PART)),
            dma((2, depth + 1, PART)),
            dma((2, depth, PART)),
            dma((2, total // 2, PART)),
            dma((2, total)),
            dma((2,)),
        ],
        compiler_params=pltpu.CompilerParams(
            collective_id=0, has_side_effects=True, vmem_limit_bytes=40 * 2**20
        ),
        name="gather_sources",
    )(scale, count, tiled(spectra))
    pick = jnp.concatenate([order, lax.axis_index("chan")[None].astype(jnp.int32)])
    block = (1, windows, channels, rows, LANES)
    stack = pl.pallas_call(
        stack_kernel,
        out_shape=jax.ShapeDtypeStruct((sources, channels, rows, LANES), bf16),
        grid_spec=pltpu.PrefetchScalarGridSpec(
            num_scalar_prefetch=1,
            grid=(total,),
            in_specs=[
                smem,
                pl.BlockSpec(block, lambda i, pick: (i, 0, 0, 0, 0)),
                pl.BlockSpec(block, lambda i, pick: (pick[sources], 0, 0, 0, 0)),
            ],
            out_specs=pl.BlockSpec((per, channels, rows, LANES), lambda i, pick: (i, 0, 0, 0)),
            scratch_shapes=[
                pltpu.VMEM((windows, channels, rows, LANES), bf16),
                pltpu.VMEM((channels, windows, rows, LANES), f32),
                pltpu.VMEM((channels, windows, rows, LANES), f32),
            ],
        ),
        compiler_params=pltpu.CompilerParams(vmem_limit_bytes=40 * 2**20),
        name="stack_sources",
    )(pick, weight, gathered, gathered)
    stack = stack.reshape(sources, channels, rows // 2, 2, LANES)
    stack = jnp.swapaxes(stack, 2, 3).reshape(sources, channels, 2, bins // 2)
    first = lax.axis_index("win") * mine
    window_weight = windows * lax.dynamic_slice_in_dim(weight[0], first, mine, 0)
    return (stack, window_weight)


def solution(mesh):
    placed = (P("win", "chan", None, None), P("win"), P("win", "chan"), P())
    wins, chans = mesh.shape["win"], mesh.shape["chan"]

    def chosen(spectra, window_gain, dead_mask, order):
        windows, _, _, bins = spectra.shape
        fits = wins == 2 and windows * wins == 8 and chans % 4 == 0
        fits = fits and bins % (16 * LANES) == 0 and order.shape[0] % (2 * chans) == 0
        return (fast_body if fits else body)(spectra, window_gain, dead_mask, order)

    return jax.shard_map(
        chosen,
        mesh=mesh,
        in_specs=placed,
        out_specs=(P(None, "chan", None, "win"), P("win")),
        check_vma=False,
    )
```

```python
import functools

import jax
import jax.numpy as jnp
from jax import lax
from jax.experimental import pallas as pl
from jax.experimental.pallas import tpu as pltpu
from jax.sharding import PartitionSpec as P

ITERS = 2
LANES = 128
PART = 4
MESH = pl.DeviceIdType.MESH


def solve_stack(src_re, src_im, ch_re, ch_im, cells):
    f32 = jnp.float32
    bf16 = jnp.bfloat16
    corr_form = "ksf,kcf->scf"
    proj_form = "ksf,scf->kcf"
    row_axis = 1
    freq_axis = 1
    cross_axes = (1, 2)
    count = src_re.shape[0]
    a_square = jnp.sum(
        jnp.square(src_re.astype(f32)) + jnp.square(src_im.astype(f32)), axis=row_axis
    )
    b_square = jnp.sum(jnp.square(ch_re.astype(f32)) + jnp.square(ch_im.astype(f32)), axis=row_axis)
    energy = jnp.sum(a_square * b_square, axis=freq_axis)

    def product(form, left, right):
        return jnp.einsum(form, left, right, preferred_element_type=f32)

    def stack_of(weight):
        shaped = weight[:, None, None]
        w_re = (shaped * ch_re.astype(f32)).astype(bf16)
        w_im = (shaped * ch_im.astype(f32)).astype(bf16)
        total = jnp.sum(weight)
        gre = (product(corr_form, src_re, w_re) + product(corr_form, src_im, w_im)) / total
        gim = (product(corr_form, src_re, w_im) - product(corr_form, src_im, w_re)) / total
        return (gre.astype(bf16), gim.astype(bf16))

    weight = jnp.ones((count,), f32)
    for step in range(ITERS):
        gre, gim = stack_of(weight)
        p_re = product(proj_form, src_re, gre) - product(proj_form, src_im, gim)
        p_im = product(proj_form, src_re, gim) + product(proj_form, src_im, gre)
        cross = jnp.sum(ch_re.astype(f32) * p_re + ch_im.astype(f32) * p_im, axis=cross_axes)
        power = jnp.sum(jnp.square(gre.astype(f32)) + jnp.square(gim.astype(f32)))
        partial_misfit = energy - 2.0 * cross + power
        misfit = lax.psum(partial_misfit, ("win", "chan"))
        weight = 1.0 / jnp.sqrt(misfit / cells + 1e-06)
    gre, gim = stack_of(weight)
    return (gre, gim, weight)


def body(spectra, window_gain, dead_mask, order):
    f32 = jnp.float32
    bf16 = jnp.bfloat16
    scaled = (
        dead_mask.astype(f32)[:, :, None, None]
        * window_gain[:, None, None, None]
        * spectra.astype(f32)
    ).astype(bf16)
    sources = order.shape[0]
    per_dev = sources // lax.axis_size("chan")
    channels = spectra.shape[1]
    cells = sources * channels * lax.axis_size("chan") * spectra.shape[3]
    local = lax.all_to_all(scaled, "win", split_axis=3, concat_axis=0, tiled=True)
    first = lax.axis_index("chan") * per_dev
    mine = lax.dynamic_slice_in_dim(order, first, per_dev, 0)
    picked = jnp.take(local, mine, axis=1)
    gathered = lax.all_gather(picked, "chan", axis=1, tiled=True)
    gre, gim, weight = solve_stack(
        gathered[:, :, 0, :], gathered[:, :, 1, :], local[:, :, 0, :], local[:, :, 1, :], cells
    )
    stack = jnp.stack([gre, gim], axis=2)
    count = weight.shape[0]
    normed = weight * (count / jnp.sum(weight))
    first_window = lax.axis_index("win") * spectra.shape[0]
    window_weight = lax.dynamic_slice_in_dim(normed, first_window, spectra.shape[0], 0)
    return (stack, window_weight)


def even_rows(shape):
    return lax.rem(lax.broadcasted_iota(jnp.int32, shape, len(shape) - 2), 2) == 0


def next_row(x):
    return pltpu.roll(x, x.shape[0] - 1, 0)


def prev_row(x):
    return pltpu.roll(x, 1, 0)


def swapped(x, even):
    return jnp.where(even, next_row(x), prev_row(x))


def gather_kernel(
    cells,
    scale_ref,
    count_ref,
    spectra_ref,
    out_ref,
    weight_ref,
    held,
    away,
    grams,
    lines,
    sums,
    halves,
    out_sems,
    x_sems,
    up_sems,
    down_sems,
    y_sems,
    rise_sems,
    fall_sems,
    pair_sems,
    sum_sems,
    half_sems,
):
    f32 = jnp.float32
    bf16 = jnp.bfloat16
    total = lax.axis_size("chan")
    depth = total // 4
    me = lax.axis_index("chan")
    win = lax.axis_index("win")
    core = lax.rem(me, 2)
    row = lax.rem(me // 2, 2)
    level = me // 4
    windows, channels, rows = held.shape[1], held.shape[2], held.shape[3]
    mine = windows // 2
    step_windows = windows // PART
    other = {"win": 1 - win}

    def place(z, y):
        return (z * 2 + y) * 2 + core

    barrier = pltpu.get_barrier_semaphore()

    @pl.loop(1, total)
    def _(i):
        pl.semaphore_signal(
            barrier, inc=1, device_id={"chan": lax.rem(me + i, total)}, device_id_type=MESH
        )

    pl.semaphore_signal(barrier, inc=1, device_id=other, device_id_type=MESH)

    def prepare(kept):
        for half in range(2):

            @pl.when(win == half)
            def _():
                part = half if kept else 1 - half

                @pl.loop(0, channels, unroll=4)
                def _(c):
                    for k in range(mine):
                        value = spectra_ref[k, c, part * rows : (part + 1) * rows, :].astype(f32)
                        value = (scale_ref[k, c] * value).astype(bf16)
                        if kept:
                            held[me, half * mine + k, c] = value
                        else:
                            away[k, c] = value

    prepare(False)
    pl.semaphore_wait(barrier, total)

    def across(j):
        start = pl.ds(j * step_windows, step_windows)
        return pltpu.make_async_remote_copy(
            src_ref=away.at[start],
            dst_ref=held.at[me, pl.ds(win * mine + j * step_windows, step_windows)],
            send_sem=x_sems.at[0, j],
            recv_sem=x_sems.at[1, j],
            device_id=other,
            device_id_type=MESH,
        )

    for j in range(PART // 2):
        across(j).start()
    prepare(True)

    def piece(block, q):
        return held.at[block, pl.ds(q * step_windows, step_windows)]

    def send(block, q, sems, slot_out, slot_in, target):
        return pltpu.make_async_remote_copy(
            src_ref=piece(block, q),
            dst_ref=piece(block, q),
            send_sem=sems.at[0, slot_out, q],
            recv_sem=sems.at[1, slot_in, q],
            device_id={"chan": target},
            device_id_type=MESH,
        )

    sibling = me + 1 - 2 * core

    def up(block, q, t):
        return send(block, q, up_sems, t, t + 1, lax.rem(me + 4, total))

    def down(block, q, t):
        return send(block, q, down_sems, t, t + 1, lax.rem(me + total - 4, total))

    def rise(block, q, t):
        return send(block, q, rise_sems, t, t + 1, lax.rem(me + 4, total))

    def fall(block, q, t):
        return send(block, q, fall_sems, t, t + 1, lax.rem(me + total - 4, total))

    def cross(z, q):
        return send(place(z, row), q, y_sems, z, z, place(level, 1 - row))

    def pair(block, q):
        return send(block, q, pair_sems, block // 2, block // 2, sibling)

    def arrive(block, q, sems, slot):
        send(block, q, sems, slot, slot, sibling).wait_recv()

    def each(t, act):
        if t == 0:
            act(level, True, True)
        else:

            @pl.when(level - t >= 0)
            def _():
                act(level - t, True, False)

            @pl.when(level + t < depth)
            def _():
                act(level + t, False, True)

    def spread(t, q, late, act):
        def one(z, rising, falling):
            block = place(z, row)
            if t > 0:
                if act == "start":
                    arrive(block, q, up_sems if rising else down_sems, t)
            run = lambda copy: copy.start() if act == "start" else copy.wait_send()
            if rising and t < depth - 1:

                @pl.when(level < depth - 1)
                def _():
                    run(up(block, q, t))

            if falling and t < depth - 1:

                @pl.when(level > 0)
                def _():
                    run(down(block, q, t))

            if t == 0:
                run(cross(z, q))
            else:

                @pl.when(jnp.logical_not(late))
                def _():
                    run(cross(z, q))

            run(pair(block, q))

        each(t, one)

    def receive_cross(t, q, late, act):
        def one(z, rising, falling):
            block = place(z, 1 - row)
            run = lambda copy: copy.start() if act == "start" else copy.wait_send()
            if act == "start":
                if t == 0:
                    arrive(block, q, y_sems, z)
                else:

                    @pl.when(late)
                    def _():
                        arrive(block, q, rise_sems if rising else fall_sems, t)

                    @pl.when(jnp.logical_not(late))
                    def _():
                        arrive(block, q, y_sems, z)

            if rising and t < depth - 1:

                @pl.when(jnp.logical_and(late, level < depth - 1))
                def _():
                    run(rise(block, q, t))

            if falling and t < depth - 1:

                @pl.when(jnp.logical_and(late, level > 0))
                def _():
                    run(fall(block, q, t))

            run(pair(block, q))

        each(t, one)

    even = even_rows((rows, LANES))
    for k in range(windows):
        for j in range(k, windows):
            for form in range(2):
                grams[0, form, k * windows + j] = jnp.zeros((rows, LANES), f32)
                grams[1, form, k * windows + j] = jnp.zeros((rows, LANES), f32)

    def gram(which, block, factors):
        for k in range(windows):
            zero = jnp.zeros((rows, LANES), f32)

            def add(c, carry):
                plain, turned = carry
                x = held[block, k, c].astype(f32) * count_ref[factors, c]
                y = swapped(x, even)
                new_plain, new_turned = [], []
                for j in range(k, windows):
                    z = held[block, j, c].astype(f32)
                    new_plain.append(plain[j - k] + x * z)
                    if j > k:
                        new_turned.append(turned[j - k - 1] + y * z)
                return tuple(new_plain), tuple(new_turned)

            span = (zero,) * (windows - k)
            plain, turned = lax.fori_loop(0, channels, add, (span, span[1:]), unroll=4)
            for j in range(k, windows):
                grams[which, 0, k * windows + j] += plain[j - k]
                if j > k:
                    grams[which, 1, k * windows + j] += turned[j - k - 1]

    def copy_out(block):
        return pltpu.make_async_copy(held.at[block], out_ref.at[block], out_sems.at[block])

    def settle(t, y, theirs):
        def one(z, rising, falling):
            mate = place(z, y)
            block = mate + theirs * (1 - 2 * core)

            @pl.when(theirs == 1)
            def _():
                for q in range(PART):
                    arrive(block, q, pair_sems, block // 2)

            copy_out(block).start()
            gram(0, block, block)

        if t >= 0:
            each(t, one)

    for t in range(depth + 1):

        @pl.loop(0, PART)
        def _(p):
            q = lax.rem(p + win * (PART // 2), PART)
            if t == 0:

                @pl.when(p >= PART // 2)
                def _():
                    across(p - PART // 2).wait_recv()

            if t < depth:
                spread(t, q, p == PART - 1, "start")
            if t > 0:
                receive_cross(t - 1, q, p == PART - 1, "start")

                @pl.when(p < 2)
                def _():
                    settle(t - 1, row, p)

                @pl.when(p >= 2)
                def _():
                    settle(t - 2, 1 - row, p - 2)

        if t == 0:
            gram(1, me, total)

    @pl.loop(0, 2)
    def _(p):
        settle(depth - 1, 1 - row, p)

    for k in range(windows):
        for j in range(k, windows):
            at = k * windows + j
            value = jnp.zeros((rows, LANES), f32)
            for form in range(2):
                a, b = grams[0, form, at], grams[1, form, at]
                sign = 1.0 if form == 0 else -1.0
                value += (a + sign * next_row(a)) * (b + sign * next_row(b))
            line = jnp.sum(jnp.where(even, value, 0.0), axis=0, keepdims=True)
            lines[k, j : j + 1, :] = line
            lines[j, k : k + 1, :] = line

    lane = lax.broadcasted_iota(jnp.int32, (windows, LANES), 1)
    sub = lax.broadcasted_iota(jnp.int32, (windows, LANES), 0)
    part = jnp.zeros((windows, LANES), f32)
    for k in range(windows):
        part = jnp.where(lane == k, jnp.sum(lines[k], axis=1, keepdims=True), part)
    sums[me] = part

    def share(i):
        target = lax.rem(me + i, total)
        return pltpu.make_async_remote_copy(
            src_ref=sums.at[me],
            dst_ref=sums.at[me],
            send_sem=sum_sems.at[0, target],
            recv_sem=sum_sems.at[1, me],
            device_id={"chan": target},
            device_id_type=MESH,
        )

    @pl.loop(1, total)
    def _(i):
        share(i).start()

    @pl.loop(1, total)
    def _(i):
        source = lax.rem(me + i, total)
        pltpu.make_async_remote_copy(
            src_ref=sums.at[source],
            dst_ref=sums.at[source],
            send_sem=sum_sems.at[0, source],
            recv_sem=sum_sems.at[1, source],
            device_id={"chan": source},
            device_id_type=MESH,
        ).wait_recv()

    group = sums[0]
    for i in range(1, total):
        group = group + sums[i]
    halves[0] = group
    trade = pltpu.make_async_remote_copy(
        src_ref=halves.at[0],
        dst_ref=halves.at[1],
        send_sem=half_sems.at[0],
        recv_sem=half_sems.at[1],
        device_id=other,
        device_id_type=MESH,
    )
    trade.start()
    trade.wait_recv()
    table = halves[0] + halves[1]
    diagonal = lane == sub
    energy = jnp.sum(jnp.where(diagonal, table, 0.0), axis=0, keepdims=True)
    live = lane[:1] < windows
    weight = jnp.where(live, 1.0, 0.0)
    for _ in range(ITERS):
        column = jnp.sum(jnp.where(diagonal, weight, 0.0), axis=1, keepdims=True)
        total_weight = jnp.sum(weight, axis=1, keepdims=True)
        cross_row = jnp.sum(table * column, axis=0, keepdims=True) / total_weight
        power = jnp.sum(weight * cross_row, axis=1, keepdims=True) / total_weight
        misfit = energy - 2.0 * cross_row + power
        weight = jnp.where(live, 1.0 / jnp.sqrt(misfit / cells + 1e-06), 0.0)
    weight_ref[...] = weight / jnp.sum(weight, axis=1, keepdims=True)

    for j in range(PART // 2):
        across(j).wait_send()
    for t in range(depth + 1):

        @pl.loop(0, PART)
        def _(p):
            q = lax.rem(p + win * (PART // 2), PART)
            if t < depth:
                spread(t, q, p == PART - 1, "end")
            if t > 0:
                receive_cross(t - 1, q, p == PART - 1, "end")

    @pl.loop(1, total)
    def _(i):
        share(i).wait_send()

    trade.wait_send()

    @pl.loop(0, total)
    def _(i):
        copy_out(i).wait()


def stack_kernel(pick_ref, weight_ref, source_ref, own_ref, out_ref, turned, first, second):
    f32 = jnp.float32
    bf16 = jnp.bfloat16
    windows, channels, rows = turned.shape[0], turned.shape[1], turned.shape[2]
    step = pl.program_id(0)
    even = even_rows((rows, LANES))
    per = out_ref.shape[0]

    @pl.when(step == 0)
    def _():
        for k in range(windows):

            @pl.loop(0, channels)
            def _(c):
                x = own_ref[0, k, c].astype(f32) * weight_ref[0, k]
                x = x.astype(bf16).astype(f32)
                first[c, k] = jnp.where(even, x, -prev_row(x))
                second[c, k] = jnp.where(even, next_row(x), x)

    for k in range(windows):

        @pl.loop(0, channels, unroll=16)
        def _(c):
            x = source_ref[0, k, c].astype(f32)
            turned[k, c] = swapped(x, even).astype(bf16)

    @pl.loop(0, per)
    def _(s):
        i = pick_ref[step * per + s]
        a = [source_ref[0, k, i].astype(f32) for k in range(windows)]
        t = [turned[k, i].astype(f32) for k in range(windows)]

        @pl.loop(0, channels, unroll=16)
        def _(c):
            value = None
            for k in range(windows):
                term = a[k] * first[c, k] + t[k] * second[c, k]
                value = term if value is None else value + term
            out_ref[s, c] = value.astype(bf16)


def tiled(x):
    lead, bins = x.shape[:-2], x.shape[-1]
    x = x.reshape(*lead, 2, bins // LANES, LANES)
    return jnp.swapaxes(x, -3, -2).reshape(*lead, bins // LANES * 2, LANES)


def fast_body(spectra, window_gain, dead_mask, order):
    f32 = jnp.float32
    bf16 = jnp.bfloat16
    total = lax.axis_size("chan")
    mine, channels, _, bins = spectra.shape
    windows = mine * 2
    rows = bins // LANES
    sources = order.shape[0]
    per = sources // total
    cells = float(sources * channels * total * bins)
    scale = dead_mask.astype(f32) * window_gain[:, None]
    hits = order.reshape(total, per, 1) == jnp.arange(channels, dtype=jnp.int32)
    count = jnp.sum(hits.astype(f32), axis=1)
    count = jnp.concatenate([count, jnp.ones((1, channels), f32)], axis=0)
    smem = pl.BlockSpec(memory_space=pltpu.SMEM)
    vmem = pl.BlockSpec(memory_space=pltpu.VMEM)
    dma = pltpu.SemaphoreType.DMA
    depth = total // 4
    gathered, weight = pl.pallas_call(
        functools.partial(gather_kernel, cells),
        out_shape=(
            jax.ShapeDtypeStruct((total, windows, channels, rows, LANES), bf16),
            jax.ShapeDtypeStruct((1, LANES), f32),
        ),
        in_specs=[smem, smem, vmem],
        out_specs=(pl.BlockSpec(memory_space=pl.ANY), vmem),
        scratch_shapes=[
            pltpu.VMEM((total, windows, channels, rows, LANES), bf16),
            pltpu.VMEM((mine, channels, rows, LANES), bf16),
            pltpu.VMEM((2, 2, windows * windows, rows, LANES), f32),
            pltpu.VMEM((windows, windows, LANES), f32),
            pltpu.VMEM((total, windows, LANES), f32),
            pltpu.VMEM((2, windows, LANES), f32),
            dma((total,)),
            dma((2, PART // 2)),
            dma((2, depth + 1, PART)),
            dma((2, depth + 1, PART)),
            dma((2, depth, PART)),
            dma((2, depth + 1, PART)),
            dma((2, depth + 1, PART)),
            dma((2, total // 2, PART)),
            dma((2, total)),
            dma((2,)),
        ],
        compiler_params=pltpu.CompilerParams(
            collective_id=0, has_side_effects=True, vmem_limit_bytes=40 * 2**20
        ),
        name="gather_sources",
    )(scale, count, tiled(spectra))
    pick = jnp.concatenate([order, lax.axis_index("chan")[None].astype(jnp.int32)])
    block = (1, windows, channels, rows, LANES)
    stack = pl.pallas_call(
        stack_kernel,
        out_shape=jax.ShapeDtypeStruct((sources, channels, rows, LANES), bf16),
        grid_spec=pltpu.PrefetchScalarGridSpec(
            num_scalar_prefetch=1,
            grid=(total,),
            in_specs=[
                smem,
                pl.BlockSpec(block, lambda i, pick: (i, 0, 0, 0, 0)),
                pl.BlockSpec(block, lambda i, pick: (pick[sources], 0, 0, 0, 0)),
            ],
            out_specs=pl.BlockSpec((per, channels, rows, LANES), lambda i, pick: (i, 0, 0, 0)),
            scratch_shapes=[
                pltpu.VMEM((windows, channels, rows, LANES), bf16),
                pltpu.VMEM((channels, windows, rows, LANES), f32),
                pltpu.VMEM((channels, windows, rows, LANES), f32),
            ],
        ),
        compiler_params=pltpu.CompilerParams(vmem_limit_bytes=40 * 2**20),
        name="stack_sources",
    )(pick, weight, gathered, gathered)
    stack = stack.reshape(sources, channels, rows // 2, 2, LANES)
    stack = jnp.swapaxes(stack, 2, 3).reshape(sources, channels, 2, bins // 2)
    first = lax.axis_index("win") * mine
    window_weight = windows * lax.dynamic_slice_in_dim(weight[0], first, mine, 0)
    return (stack, window_weight)


def solution(mesh):
    placed = (P("win", "chan", None, None), P("win"), P("win", "chan"), P())
    wins, chans = mesh.shape["win"], mesh.shape["chan"]

    def chosen(spectra, window_gain, dead_mask, order):
        windows, _, _, bins = spectra.shape
        fits = wins == 2 and windows * wins == 8 and chans % 4 == 0
        fits = fits and bins % (16 * LANES) == 0 and order.shape[0] % (2 * chans) == 0
        return (fast_body if fits else body)(spectra, window_gain, dead_mask, order)

    return jax.shard_map(
        chosen,
        mesh=mesh,
        in_specs=placed,
        out_specs=(P(None, "chan", None, "win"), P("win")),
        check_vma=False,
    )
```
